512 devices in a mesh: row: 4 (over z_lo), col: 8 (over x, core), dev: 16 (over z_hi, y).
Axes of the slice: x: 4, y: 8, z: 8 (z_hi: 2, z_lo: 4; z = z_hi * 4 + z_lo), core: 2. Of those that a mesh axis runs over, the one named last changes fastest.
Arguments:
- train_states: bfloat16 [512, 2, 262144], P(('row', 'col'), None, 'dev'), may hold values from -120 to 120, as said below
- test_states: bfloat16 [768, 2, 262144], P(('col', 'row'), None, 'dev'), may hold values from -120 to 120, as said below
Outputs:
- kernel: float32 [512, 768], P('row', 'col')
The draws below stay inside these ranges and needn't reach their ends.
Inputs may be any that keep to these rules, and one draw needn't show every extreme that they name: `train_states`: unnormalized states. `test_states`: unnormalized states.
All inputs are finite; a program needn't handle non-finite values.
Results may differ from the reference program's by a relative error of at most 0.0003.
Values may be sent and summed in bfloat16 or wider, within the bound.
No kernel may reach another device: no remote copies, remote signals or barrier semaphores. Data moves between devices by JAX's collectives and lax.ppermute only.
A program may use at most 64 MiB of HBM per device.

```python
import math
import jax
import jax.numpy as jnp
from jax import lax

AMPS = 262144
TRAIN = 512
TEST = 768


def amp_ramp(power):
    position = jnp.arange(AMPS).astype(jnp.float32) / (AMPS - 1)
    return (1.0 + 2.0 * position) ** power


def state_values(key, count):
    first, second = jax.random.split(key)
    scales = jnp.exp(jax.random.uniform(first, (count, 1, 1)) * math.log(10.0))
    base = jnp.clip(jax.random.normal(second, (count, 2, AMPS)), -4.0, 4.0)
    shape = amp_ramp(1.0)
    return (base * scales * shape).astype(jnp.bfloat16)


def draw_train_states(key, part):
    key = jax.random.fold_in(key, 11)
    return state_values(key, TRAIN)


def draw_test_states(key, part):
    key = jax.random.fold_in(key, 23)
    return state_values(key, TEST)


def setup_inputs(seed: int = 0) -> dict:
    key_list = jax.random.split(jax.random.key(seed), 3)
    return {
        "train_states": draw_train_states(jax.random.fold_in(key_list[2], 71), 0),
        "test_states": draw_test_states(jax.random.fold_in(key_list[2], 71), 0),
    }


def cross(left, right):
    return jnp.dot(left, right.T, preferred_element_type=jnp.float32)


def squares(states):
    return lax.map(lambda single: jnp.sum(jnp.square(single.astype(jnp.float32))), states)


def reference(train_states, test_states):
    real_a, imag_a = train_states[:, 0], train_states[:, 1]
    real_b, imag_b = test_states[:, 0], test_states[:, 1]
    real_part = cross(real_a, real_b) + cross(imag_a, imag_b)
    imag_part = cross(real_a, imag_b) - cross(imag_a, real_b)
    train_norm = squares(train_states)
    test_norm = squares(test_states)
    return AMPS * (real_part * real_part + imag_part * imag_part) / (train_norm[:, None] * test_norm[None, :])
```

```python
import functools

import jax
import jax.numpy as jnp
from jax import lax
from jax.experimental import pallas as pl
from jax.experimental.pallas import tpu as pltpu
from jax.sharding import Mesh, PartitionSpec as P

AMPS = 262144
F32 = jnp.float32
DEV = ("zhi", "y")
SPARE = 192
WINDOW = 63

PLUS = [(i, (i + 1) % 4) for i in range(4)]
MINUS = [(i, (i - 1) % 4) for i in range(4)]
SWAP = [(0, 1), (1, 0)]


def params():
    return pltpu.CompilerParams(vmem_limit_bytes=48 * 1024 * 1024)


def whole(n):
    return [pl.BlockSpec(memory_space=pltpu.VMEM)] * n


def spread(states):
    count = states.shape[0]
    cut = states.reshape(count, 2, 4, 4096).transpose(2, 1, 0, 3)
    return cut


def gather_x(own):
    left = lax.ppermute(own, "x", PLUS)
    right = lax.ppermute(own, "x", MINUS)
    far_a = lax.ppermute(left[:2], "x", PLUS)
    far_b = lax.ppermute(right[2:], "x", MINUS)
    blocks = [own, left, right, far_a, far_b]
    return blocks + [lax.ppermute(b, "core", SWAP) for b in blocks]


def rows_of(refs, lanes):
    out = []
    for core in (0, 5):
        for k in (0, 1, 2):
            r = refs[core + k]
            out.append(r[:, :, lanes].reshape(64, -1))
        a, b = refs[core + 3], refs[core + 4]
        out.append(a[:, :, lanes].reshape(32, -1))
        out.append(b[:, :, lanes].reshape(32, -1))
    return jnp.concatenate(out, axis=0)


def norm_kernel(*refs):
    u, v, out = refs[:10], refs[10:20], refs[20]
    total = jnp.zeros((512, 128), F32)
    for k in range(32):
        for part in (u, v):
            x = rows_of(part, pl.ds(128 * k, 128)).astype(F32)
            total = total + x * x
    sums = jnp.sum(total, axis=1, keepdims=True)
    lane = lax.broadcasted_iota(jnp.int32, (512, 128), 1)
    out[...] = jnp.where(lane == SPARE - 128, sums, 0.0)


def product_kernel(*refs):
    u, v, s_ref, norms, out = refs[:10], refs[10:20], refs[20], refs[21], refs[22]
    nt = (((1,), (1,)), ((), ()))
    width = 512
    gu = jnp.zeros((512, 192), F32)
    gv = jnp.zeros((512, 192), F32)
    ss = jnp.zeros((192, 192), F32)
    for k in range(4096 // width):
        lanes = pl.ds(width * k, width)
        s = s_ref[:, :, lanes].reshape(192, width)
        gu = gu + lax.dot_general(rows_of(u, lanes), s, nt, preferred_element_type=F32)
        gv = gv + lax.dot_general(rows_of(v, lanes), s, nt, preferred_element_type=F32)
        ss = ss + lax.dot_general(s, s, nt, preferred_element_type=F32)

    def pad(x):
        return jnp.concatenate([x, jnp.zeros((x.shape[0], 256 - 192), F32)], axis=1)

    gu, gv, ss = pad(gu), pad(gv), pad(ss)
    lane = lax.broadcasted_iota(jnp.int32, (512, 256), 1)
    first = (lane % 48) < 24
    both = gu + jnp.where(first, pltpu.roll(gv, 256 - 24, 1), -pltpu.roll(gv, 24, 1))
    both = jnp.where(lane < SPARE, both, 0.0)

    r = lax.broadcasted_iota(jnp.int32, (192, 256), 0)
    c = lax.broadcasted_iota(jnp.int32, (192, 256), 1)
    diag = jnp.sum(jnp.where(r == c, ss, 0.0), axis=0, keepdims=True)
    diag = jnp.broadcast_to(diag, (8, 256))
    sub = lax.broadcasted_iota(jnp.int32, (8, 256), 0)
    lane8 = lax.broadcasted_iota(jnp.int32, (8, 256), 1)
    spare = jnp.zeros((8, 256), F32)
    for w in range(4):
        moved = pltpu.roll(diag, (SPARE + 1 - WINDOW * w) % 256, 1)
        keep = (sub == w) & (lane8 > SPARE)
        spare = spare + jnp.where(keep, moved, 0.0)

    tn = jnp.concatenate([jnp.zeros((512, 128), F32), norms[...]], axis=1)
    both = (both + tn).reshape(64, 8, 256) + spare[None]
    both = both.reshape(8, 4, 2, 8, 256)
    for j in range(8):
        out[:, 2 * j : 2 * j + 2] = both[j]


def per_device(train, test):
    t = spread(train)
    s = spread(test).reshape(4, 48, 4096)
    a2a = functools.partial(lax.all_to_all, split_axis=0, concat_axis=0, tiled=True)
    u = a2a(t[:, 0], "row")
    v_in, u = lax.optimization_barrier((t[:, 1], u))
    v = a2a(v_in, "row")
    s_in, v = lax.optimization_barrier((s, v))
    s = a2a(s_in, "row")
    us, vs = gather_x(u), gather_x(v)
    norms = pl.pallas_call(
        norm_kernel,
        out_shape=jax.ShapeDtypeStruct((512, 128), F32),
        in_specs=whole(20),
        out_specs=pl.BlockSpec(memory_space=pltpu.VMEM),
        compiler_params=params(),
        name="norms",
    )(*us, *vs)
    pieces = pl.pallas_call(
        product_kernel,
        out_shape=jax.ShapeDtypeStruct((4, 16, 8, 256), F32),
        in_specs=whole(22),
        out_specs=pl.BlockSpec(memory_space=pltpu.VMEM),
        compiler_params=params(),
        name="products",
    )(*us, *vs, s, norms)
    parts = a2a(pieces.reshape(64, 8, 256), ("row",) + DEV)
    total = jnp.sum(parts, axis=0)
    g = total[:, :SPARE].reshape(8, 4, 2, 24)
    power = (g[:, :, 0] ** 2 + g[:, :, 1] ** 2).reshape(8, 96)
    tn = total[:, SPARE : SPARE + 1]
    diag = total[:4, SPARE + 1 :].reshape(4 * WINDOW)[:192].reshape(4, 2, 24)
    sn = (diag[:, 0] + diag[:, 1]).reshape(1, 96)
    block = float(AMPS) * power / (tn * sn)
    full = a2a(jnp.broadcast_to(block[None], (16, 8, 96)), DEV)
    full = full.reshape(2, 4, 16, 96)
    core, x = lax.axis_index("core"), lax.axis_index("x")
    full = jnp.where(core == 0, full, full[::-1])
    full = full[:, jnp.array([0, 2, 3, 1])]
    full = full.transpose(1, 0, 2, 3)
    full = lax.dynamic_slice_in_dim(jnp.concatenate([full, full]), (4 - x) % 4, 4, 0)
    return full.reshape(128, 96)


def solution(mesh):
    axes = ("row", "x", "core", "zhi", "y")
    fine = Mesh(mesh.devices.reshape(4, 4, 2, 2, 8), axes)
    placed = (
        P(("row", "x", "core"), None, DEV),
        P(("x", "core", "row"), None, DEV),
    )
    return jax.shard_map(
        per_device, mesh=fine, in_specs=placed, out_specs=P("row", ("x", "core")), check_vma=False
    )
```

```python
import functools

import jax
import jax.numpy as jnp
from jax import lax
from jax.experimental import pallas as pl
from jax.experimental.pallas import tpu as pltpu
from jax.sharding import Mesh, PartitionSpec as P

AMPS = 262144
F32 = jnp.float32
DEV = ("zhi", "y")
SPARE = 192
WINDOW = 63

K_STEP = 512
SWAP = [(0, 1), (1, 0)]
AROUND = [(2 * x + c, 2 * ((x + (1, -1)[c]) % 4) + c) for x in range(4) for c in (0, 1)]


def params():
    return pltpu.CompilerParams(vmem_limit_bytes=48 * 1024 * 1024)


def spread(states):
    return states.reshape(states.shape[0], 2, 4, 4096).transpose(2, 1, 0, 3)


def swap(block):
    return lax.ppermute(block, "core", SWAP)


def around(block):
    return lax.ppermute(block, ("x", "core"), AROUND)


def product_kernel(place, *refs):
    u_refs, v_refs, (s_ref, out, gu, gv, ss, tt) = refs[:6], refs[6:12], refs[12:]
    k = pl.program_id(0)
    nt = (((1,), (1,)), ((), ()))

    @pl.when(k == 0)
    def _():
        gu[...] = jnp.zeros_like(gu)
        gv[...] = jnp.zeros_like(gv)
        ss[...] = jnp.zeros_like(ss)
        tt[...] = jnp.zeros_like(tt)

    u = jnp.concatenate([r[...] for r in u_refs], axis=0).reshape(512, K_STEP)
    v = jnp.concatenate([r[...] for r in v_refs], axis=0).reshape(512, K_STEP)
    s = s_ref[...].reshape(192, K_STEP)
    gu[:, :SPARE] += lax.dot_general(u, s, nt, preferred_element_type=F32)
    gv[:, :SPARE] += lax.dot_general(v, s, nt, preferred_element_type=F32)
    ss[:, :SPARE] += lax.dot_general(s, s, nt, preferred_element_type=F32)
    total = tt[...]
    for j in range(K_STEP // 128):
        for part in (u, v):
            x = part[:, 128 * j : 128 * j + 128].astype(F32)
            total = total + x * x
    tt[...] = total

    @pl.when(k == pl.num_programs(0) - 1)
    def _():
        lane = lax.broadcasted_iota(jnp.int32, (512, 256), 1)
        first = (lane % 48) < 24
        g = gv[...]
        both = gu[...] + jnp.where(first, pltpu.roll(g, 256 - 24, 1), -pltpu.roll(g, 24, 1))
        tn = jnp.sum(tt[...], axis=1, keepdims=True)
        both = jnp.where(lane < SPARE, both, jnp.where(lane == SPARE, tn, 0.0))

        r = lax.broadcasted_iota(jnp.int32, (192, 256), 0)
        c = lax.broadcasted_iota(jnp.int32, (192, 256), 1)
        diag = jnp.sum(jnp.where(r == c, ss[...], 0.0), axis=0, keepdims=True)
        diag = jnp.broadcast_to(diag, (8, 256))
        sub = lax.broadcasted_iota(jnp.int32, (8, 256), 0)
        lane8 = lax.broadcasted_iota(jnp.int32, (8, 256), 1)
        spare = jnp.zeros((8, 256), F32)
        for w in range(4):
            moved = pltpu.roll(diag, (SPARE + 1 - WINDOW * w) % 256, 1)
            spare = spare + jnp.where((sub == w) & (lane8 > SPARE), moved, 0.0)

        both = (both.reshape(64, 8, 256) + spare[None]).reshape(8, 4, 2, 8, 256)
        for j in range(8):
            out[:, pl.ds(2 * place[j], 2)] = both[j]


def products(place, u, v, s):
    blocks = [pl.BlockSpec((b.shape[0], 16, K_STEP), lambda k: (0, 0, k)) for b in (*u, *v)]
    return pl.pallas_call(
        product_kernel,
        out_shape=jax.ShapeDtypeStruct((4, 16, 8, 256), F32),
        grid=(4096 // K_STEP,),
        in_specs=[
            pl.BlockSpec(memory_space=pltpu.SMEM),
            *blocks,
            pl.BlockSpec((4, 48, K_STEP), lambda k: (0, 0, k)),
        ],
        out_specs=pl.BlockSpec((4, 16, 8, 256), lambda k: (0, 0, 0, 0)),
        scratch_shapes=[
            pltpu.VMEM((512, 256), F32),
            pltpu.VMEM((512, 256), F32),
            pltpu.VMEM((192, 256), F32),
            pltpu.VMEM((512, 128), F32),
        ],
        compiler_params=params(),
        name="products",
    )(place, *u, *v, s)


def per_device(train, test):
    t = spread(train)
    s = spread(test).reshape(4, 48, 4096)
    a2a = functools.partial(lax.all_to_all, split_axis=0, concat_axis=0, tiled=True)
    u = a2a(t[:, 0], "row")
    v_in, u = lax.optimization_barrier((t[:, 1], u))
    v = a2a(v_in, "row")
    u_other = swap(u)
    s_in, v, u_other = lax.optimization_barrier((s, v, u_other))
    s = a2a(s_in, "row")
    v_other = swap(v)

    def gather(own, other):
        near = around(jnp.concatenate([own, other]))
        far = around(near[:4])
        return own, other, near, swap(near), far, swap(far)

    x, core = lax.axis_index("x"), lax.axis_index("core")
    step = 1 - 2 * core
    x_of = jnp.stack([x, x, x - step, x - step, x + step, x + step, x + 2, x + 2]) % 4
    core_of = jnp.stack([core, 1 - core, core, 1 - core, 1 - core, core, core, 1 - core])
    place = (2 * x_of + core_of).astype(jnp.int32)
    pieces = products(place, gather(u, u_other), gather(v, v_other), s)
    parts = a2a(pieces.reshape(64, 8, 256), ("row",) + DEV)
    total = jnp.sum(parts, axis=0)
    g = total[:, :SPARE].reshape(8, 4, 2, 24)
    power = (g[:, :, 0] ** 2 + g[:, :, 1] ** 2).reshape(8, 96)
    tn = total[:, SPARE : SPARE + 1]
    diag = total[:4, SPARE + 1 :].reshape(4 * WINDOW)[:192].reshape(4, 2, 24)
    sn = (diag[:, 0] + diag[:, 1]).reshape(1, 96)
    block = float(AMPS) * power / (tn * sn)
    full = a2a(jnp.broadcast_to(block[None], (16, 8, 96)), DEV)
    return full.reshape(128, 96)


def solution(mesh):
    axes = ("row", "x", "core", "zhi", "y")
    fine = Mesh(mesh.devices.reshape(4, 4, 2, 2, 8), axes)
    placed = (
        P(("row", "x", "core"), None, DEV),
        P(("x", "core", "row"), None, DEV),
    )
    return jax.shard_map(
        per_device, mesh=fine, in_specs=placed, out_specs=P("row", ("x", "core")), check_vma=False
    )
```

```python
import functools

import jax
import jax.numpy as jnp
from jax import lax
from jax.experimental import pallas as pl
from jax.experimental.pallas import tpu as pltpu
from jax.sharding import Mesh, PartitionSpec as P

AMPS = 262144
F32 = jnp.float32
DEV = ("zhi", "y")
SPARE = 192
WINDOW = 63

GROUP = 8
DEPTH = 2048
SWAP = [(0, 1), (1, 0)]
AHEAD, BACK = ([(2 * x + c, 2 * ((x + way[c]) % 4) + c) for x in range(4) for c in (0, 1)] for way in ((1, -1), (-1, 1)))


def params(mib):
    return pltpu.CompilerParams(vmem_limit_bytes=mib * 1024 * 1024)


def spread_kernel(states, out):
    for j in range(out.shape[0]):
        out[j] = states[:, :, DEPTH * j : DEPTH * (j + 1)].reshape(out.shape[1:])


def spread(states, mib):
    count = states.shape[0]
    return pl.pallas_call(
        spread_kernel,
        out_shape=jax.ShapeDtypeStruct((8, 2 * count, DEPTH), states.dtype),
        grid=(2,),
        in_specs=[pl.BlockSpec((count, 2, 4 * DEPTH), lambda g: (0, 0, g))],
        out_specs=pl.BlockSpec((4, 2 * count, DEPTH), lambda g: (g, 0, 0)),
        compiler_params=params(mib),
        name="spread",
    )(states)


def product_kernel(sizes, place, *refs):
    m = len(sizes)
    s_all, (keep, send, gg, tt) = refs[m], refs[-4:]
    core = place[2 * sum(sizes)]
    nt = (((1,), (1,)), ((), ()))
    starts = [sum(sizes[:i]) for i in range(m + 1)]
    columns, spare = [], []
    sub = lax.broadcasted_iota(jnp.int32, (8, 256), 0)
    lane8 = lax.broadcasted_iota(jnp.int32, (8, 256), 1)
    r = lax.broadcasted_iota(jnp.int32, (192, 192), 0)
    on = r == lax.broadcasted_iota(jnp.int32, (192, 192), 1)
    for of in (core, 1 - core):
        s = jnp.concatenate([s_all[pl.ds(2 * z + of, 1)] for z in range(4)], axis=0).reshape(192, DEPTH)
        columns.append(s)
        ss = lax.dot_general(s, s, nt, preferred_element_type=F32)
        diag = jnp.sum(jnp.where(on, ss, 0.0), axis=0, keepdims=True)
        diag = jnp.broadcast_to(jnp.concatenate([diag, jnp.zeros((1, 64), F32)], axis=1), (8, 256))
        rows = jnp.zeros((8, 256), F32)
        for w in range(4):
            moved = pltpu.roll(diag, (SPARE + 1 - WINDOW * w) % 256, 1)
            rows = rows + jnp.where((sub == w) & (lane8 > SPARE), moved, 0.0)
        spare.append(rows)

    done = 0
    while done < m:
        last = done + 1
        while last < m and starts[last] - starts[done] < GROUP:
            last += 1
        a, n = starts[done], starts[last] - starts[done]
        t = jnp.concatenate([ref[...] for ref in refs[done:last]], axis=0).reshape(32 * n, DEPTH)
        done = last
        total = jnp.zeros((32 * n, 128), F32)
        for j in range(DEPTH // 128):
            x = t[:, 128 * j : 128 * j + 128].astype(F32)
            total = total + x * x
        at = pl.ds(32 * a, 32 * n)
        tt[at, :] = total
        even, odd = pl.ds(32 * a, 16 * n, stride=2), pl.ds(32 * a + 1, 16 * n, stride=2)
        tn = jnp.sum(tt[even, :] + tt[odd, :], axis=1, keepdims=True)
        lane = lax.broadcasted_iota(jnp.int32, (16 * n, 256), 1)
        first = lane % 2 == 0
        for c, out in enumerate((keep, send)):
            g = lax.dot_general(t, columns[c], nt, preferred_element_type=F32)
            gg[2 * c, at, :] = g[:, :128]
            gg[2 * c + 1, at, :] = jnp.concatenate([g[:, 128:], jnp.zeros((32 * n, 64), F32)], axis=1)
            gu, gv = (jnp.concatenate([gg[2 * c, rows, :], gg[2 * c + 1, rows, :]], axis=1) for rows in (even, odd))
            both = gu + jnp.where(first, pltpu.roll(gv, 255, 1), -pltpu.roll(gv, 1, 1))
            both = jnp.where(lane < SPARE, both, jnp.where(lane == SPARE, tn, 0.0))
            both = (both.reshape(2 * n, 8, 256) + spare[c][None]).reshape(n, 2, 8, 256)
            for j in range(n):
                out[pl.ds(place[a + j], 1), pl.ds(place[sum(sizes) + a + j], 2)] = both[j : j + 1]


def products(at, core, blocks, s):
    n = len(at)
    place = jnp.stack([r for _, r, _ in at] + [4 * x + 2 * c for x, _, c in at] + [core]).astype(jnp.int32)
    out = pl.BlockSpec((4, 16, 8, 256), lambda k, place: (0, 0, 0, 0))
    return pl.pallas_call(
        functools.partial(product_kernel, [b.shape[0] for b in blocks]),
        out_shape=[jax.ShapeDtypeStruct((4, 16, 8, 256), F32)] * 2,
        grid_spec=pltpu.PrefetchScalarGridSpec(
            num_scalar_prefetch=1,
            grid=(1,),
            in_specs=[pl.BlockSpec(memory_space=pltpu.VMEM)] * (len(blocks) + 1),
            out_specs=[out] * 2,
            scratch_shapes=[
                pltpu.VMEM((4, 32 * n, 128), F32),
                pltpu.VMEM((32 * n, 128), F32),
            ],
        ),
        cost_estimate=pl.CostEstimate(flops=2 * 32 * n * 384 * DEPTH, bytes_accessed=64 * n * DEPTH, transcendentals=0),
        compiler_params=params(24),
        name="products",
    )(place, *blocks, s)


def per_device(train, test):
    a2a = functools.partial(lax.all_to_all, split_axis=0, concat_axis=0, tiled=True)
    x, core, row = lax.axis_index("x"), lax.axis_index("core"), lax.axis_index("row")
    held = spread(train, 60)
    t = a2a(held, ("row", "core"))

    def around(own):
        first = lax.ppermute(own, ("x", "core"), AHEAD)
        return first, lax.ppermute(own, ("x", "core"), BACK), lax.ppermute(first, ("x", "core"), AHEAD)

    mine, theirs = (lax.dynamic_slice_in_dim(held, 2 * row + c, 1, 0) for c in (core, 1 - core))
    stay = around(jnp.concatenate([mine, lax.ppermute(theirs, "core", SWAP)]))
    s, t, stay = lax.optimization_barrier((spread(test, 16), t, jnp.concatenate(stay)))
    s = a2a(s, ("row", "core"))
    others = [(row + k) % 4 for k in (1, 2, 3)]
    come = around(jnp.concatenate([lax.dynamic_slice_in_dim(t, 2 * r, 2, 0) for r in others]))
    stay_at = [(row, core), (row, 1 - core)]
    come_at = [(r, c) for r in others for c in (0, 1)]
    at = [(x, r, c) for r in range(4) for c in (0, 1)]
    for there in (stay_at, come_at):
        at += [((x + dx + 4) % 4, r, c) for dx in (2 * core - 1, 1 - 2 * core, 2) for r, c in there]
    keep, send = products(at, core, (t, stay, *come), s)
    pieces = keep + lax.ppermute(send, "core", SWAP)
    parts = a2a(pieces.reshape(64, 8, 256), ("row",) + DEV)
    total = jnp.sum(parts, axis=0)
    power = jnp.sum((total[:, :SPARE] ** 2).reshape(8, 96, 2), axis=2)
    tn = total[:, SPARE : SPARE + 1]
    diag = total[:4, SPARE + 1 :].reshape(4 * WINDOW)[:192]
    sn = jnp.sum(diag.reshape(1, 96, 2), axis=2)
    block = float(AMPS) * power / (tn * sn)
    full = a2a(jnp.broadcast_to(block[None], (16, 8, 96)), DEV)
    return full.reshape(128, 96)


def solution(mesh):
    axes = ("row", "x", "core", "zhi", "y")
    fine = Mesh(mesh.devices.reshape(4, 4, 2, 2, 8), axes)
    placed = (
        P(("row", "x", "core"), None, DEV),
        P(("x", "core", "row"), None, DEV),
    )
    return jax.shard_map(
        per_device, mesh=fine, in_specs=placed, out_specs=P("row", ("x", "core")), check_vma=False
    )
```

```python
import functools

import jax
import jax.numpy as jnp
from jax import lax
from jax.experimental import pallas as pl
from jax.experimental.pallas import tpu as pltpu
from jax.sharding import Mesh, PartitionSpec as P

AMPS = 262144
F32 = jnp.float32
DEV = ("zhi", "y")
SPARE = 192
WINDOW = 63

GROUP = 7
DEPTH = 4096
SWAP = [(0, 1), (1, 0)]
AHEAD, BACK = ([(2 * x + c, 2 * ((x + way[c]) % 4) + c) for x in range(4) for c in (0, 1)] for way in ((1, -1), (-1, 1)))


def params(mib):
    return pltpu.CompilerParams(vmem_limit_bytes=mib * 1024 * 1024)


def spread_kernel(states, out):
    for j in range(out.shape[0]):
        out[j] = states[:, :, DEPTH * j : DEPTH * (j + 1)].reshape(out.shape[1:])


def spread(states, mib):
    count = states.shape[0]
    return pl.pallas_call(
        spread_kernel,
        out_shape=jax.ShapeDtypeStruct((4, 2 * count, DEPTH), states.dtype),
        grid=(2,),
        in_specs=[pl.BlockSpec((count, 2, 2 * DEPTH), lambda g: (0, 0, g))],
        out_specs=pl.BlockSpec((2, 2 * count, DEPTH), lambda g: (g, 0, 0)),
        compiler_params=params(mib),
        name="spread",
    )(states)


def product_kernel(sizes, place, *refs):
    m = len(sizes)
    s_ref, (out, gg, tt, late, sem) = refs[m], refs[-5:]
    nt = (((1,), (1,)), ((), ()))
    starts = [sum(sizes[:i]) for i in range(m + 1)]
    held, copies = list(refs[:2]), [None, None]
    for i in range(2, m):
        held.append(late.at[pl.ds(starts[i] - starts[2], sizes[i])])
        copies.append(pltpu.make_async_copy(refs[i], held[i], sem.at[i - 2]))
    for copy in copies[2:]:
        copy.start()
    s = s_ref[...].reshape(192, DEPTH)
    ss = lax.dot_general(s, s, nt, preferred_element_type=F32)
    r = lax.broadcasted_iota(jnp.int32, (192, 192), 0)
    on = r == lax.broadcasted_iota(jnp.int32, (192, 192), 1)
    diag = jnp.sum(jnp.where(on, ss, 0.0), axis=0, keepdims=True)
    diag = jnp.broadcast_to(jnp.concatenate([diag, jnp.zeros((1, 64), F32)], axis=1), (8, 256))
    sub = lax.broadcasted_iota(jnp.int32, (8, 256), 0)
    lane8 = lax.broadcasted_iota(jnp.int32, (8, 256), 1)
    spare = jnp.zeros((8, 256), F32)
    for w in range(4):
        moved = pltpu.roll(diag, (SPARE + 1 - WINDOW * w) % 256, 1)
        spare = spare + jnp.where((sub == w) & (lane8 > SPARE), moved, 0.0)

    done = 0
    while done < m:
        last = done + 1
        while last < m and starts[last] - starts[done] < GROUP:
            last += 1
        a, n = starts[done], starts[last] - starts[done]
        for copy in copies[done:last]:
            if copy is not None:
                copy.wait()
        t = jnp.concatenate([ref[...] for ref in held[done:last]], axis=0).reshape(32 * n, DEPTH)
        done = last
        total = jnp.zeros((32 * n, 128), F32)
        for j in range(DEPTH // 128):
            x = t[:, 128 * j : 128 * j + 128].astype(F32)
            total = total + x * x
        at = pl.ds(32 * a, 32 * n)
        tt[at, :] = total
        even, odd = pl.ds(32 * a, 16 * n, stride=2), pl.ds(32 * a + 1, 16 * n, stride=2)
        tn = jnp.sum(tt[even, :] + tt[odd, :], axis=1, keepdims=True)
        lane = lax.broadcasted_iota(jnp.int32, (16 * n, 256), 1)
        first = lane % 2 == 0
        g = lax.dot_general(t, s, nt, preferred_element_type=F32)
        gg[0, at, :] = g[:, :128]
        gg[1, at, :] = jnp.concatenate([g[:, 128:], jnp.zeros((32 * n, 64), F32)], axis=1)
        gu, gv = (jnp.concatenate([gg[0, rows, :], gg[1, rows, :]], axis=1) for rows in (even, odd))
        both = gu + jnp.where(first, pltpu.roll(gv, 255, 1), -pltpu.roll(gv, 1, 1))
        both = jnp.where(lane < SPARE, both, jnp.where(lane == SPARE, tn, 0.0))
        both = (both.reshape(2 * n, 8, 256) + spare[None]).reshape(n, 2, 8, 256)
        for j in range(n):
            out[pl.ds(place[a + j], 1), pl.ds(place[sum(sizes) + a + j], 2)] = both[j : j + 1]


def products(at, blocks, s):
    n = len(at)
    place = jnp.stack([r for _, r, _ in at] + [4 * x + 2 * c for x, _, c in at]).astype(jnp.int32)
    out = pl.BlockSpec((4, 16, 8, 256), lambda k, place: (0, 0, 0, 0))
    return pl.pallas_call(
        functools.partial(product_kernel, [b.shape[0] for b in blocks]),
        out_shape=jax.ShapeDtypeStruct((4, 16, 8, 256), F32),
        grid_spec=pltpu.PrefetchScalarGridSpec(
            num_scalar_prefetch=1,
            grid=(1,),
            in_specs=[
                *[pl.BlockSpec(memory_space=pltpu.VMEM)] * 2,
                *[pl.BlockSpec(memory_space=pl.ANY)] * (len(blocks) - 2),
                pl.BlockSpec(memory_space=pltpu.VMEM),
            ],
            out_specs=out,
            scratch_shapes=[
                pltpu.VMEM((2, 32 * n, 128), F32),
                pltpu.VMEM((32 * n, 128), F32),
                pltpu.VMEM((n - blocks[0].shape[0] - blocks[1].shape[0], 32, DEPTH), jnp.bfloat16),
                pltpu.SemaphoreType.DMA((len(blocks) - 2,)),
            ],
        ),
        cost_estimate=pl.CostEstimate(flops=2 * 32 * n * 192 * DEPTH, bytes_accessed=64 * n * DEPTH, transcendentals=0),
        compiler_params=params(24),
        name="products",
    )(place, *blocks, s)


def per_device(train, test):
    a2a = functools.partial(lax.all_to_all, split_axis=0, concat_axis=0, tiled=True)
    x, core, row = lax.axis_index("x"), lax.axis_index("core"), lax.axis_index("row")
    held = spread(train, 60)
    t = a2a(held, "row")

    def swap(block):
        return lax.ppermute(block, "core", SWAP)

    def around(own):
        first = lax.ppermute(own, ("x", "core"), AHEAD)
        return first, lax.ppermute(own, ("x", "core"), BACK), lax.ppermute(first, ("x", "core"), AHEAD)

    stay = around(lax.dynamic_slice_in_dim(held, row, 1, 0))
    s, t, stay = lax.optimization_barrier((spread(test, 16), t, jnp.concatenate(stay)))
    s = a2a(s, "row")
    others = [(row + k) % 4 for k in (1, 2, 3)]
    come = around(jnp.concatenate([lax.dynamic_slice_in_dim(t, r, 1, 0) for r in others]))
    parts = [(t, range(4), (0,)), (stay, [row], (-1, 1, 2))] + [(b, others, (w,)) for b, w in zip(come, (-1, 1, 2))]
    entries = []
    for block, rows, ways in parts:
        for b, c, sign in ((block, core, 1 - 2 * core), (swap(block), 1 - core, 2 * core - 1)):
            entries.append((b, [((x + way * sign + 4) % 4, r, c) for way in ways for r in rows]))
    entries = [entries[i] for i in (0, 2, 1, 3, 4, 5, 6, 7, 8, 9)]
    blocks, at = [b for b, _ in entries], [place for _, places in entries for place in places]
    pieces = products(at, blocks, s)
    parts = a2a(pieces.reshape(64, 8, 256), ("row",) + DEV)
    total = jnp.sum(parts, axis=0)
    power = jnp.sum((total[:, :SPARE] ** 2).reshape(8, 96, 2), axis=2)
    tn = total[:, SPARE : SPARE + 1]
    diag = total[:4, SPARE + 1 :].reshape(4 * WINDOW)[:192]
    sn = jnp.sum(diag.reshape(1, 96, 2), axis=2)
    block = float(AMPS) * power / (tn * sn)
    full = a2a(jnp.broadcast_to(block[None], (16, 8, 96)), DEV)
    return full.reshape(128, 96)


def solution(mesh):
    axes = ("row", "x", "core", "zhi", "y")
    fine = Mesh(mesh.devices.reshape(4, 4, 2, 2, 8), axes)
    placed = (
        P(("row", "x", "core"), None, DEV),
        P(("x", "core", "row"), None, DEV),
    )
    return jax.shard_map(
        per_device, mesh=fine, in_specs=placed, out_specs=P("row", ("x", "core")), check_vma=False
    )
```

```python
import functools

import jax
import jax.numpy as jnp
from jax import lax
from jax.experimental import pallas as pl
from jax.experimental.pallas import tpu as pltpu
from jax.sharding import Mesh, PartitionSpec as P

AMPS = 262144
F32 = jnp.float32
DEV = ("zhi", "y")
SPARE = 192
WINDOW = 63

GROUP = 7
DEPTH = 4096
SWAP = [(0, 1), (1, 0)]
AHEAD, BACK = ([(2 * x + c, 2 * ((x + way[c]) % 4) + c) for x in range(4) for c in (0, 1)] for way in ((1, -1), (-1, 1)))


def params(mib):
    return pltpu.CompilerParams(vmem_limit_bytes=mib * 1024 * 1024)


def spread_kernel(states, out):
    for j in range(out.shape[0]):
        out[j] = states[:, :, DEPTH * j : DEPTH * (j + 1)].reshape(out.shape[1:])


def spread(states, mib):
    count = states.shape[0]
    return pl.pallas_call(
        spread_kernel,
        out_shape=jax.ShapeDtypeStruct((4, 2 * count, DEPTH), states.dtype),
        grid=(2,),
        in_specs=[pl.BlockSpec((count, 2, 2 * DEPTH), lambda g: (0, 0, g))],
        out_specs=pl.BlockSpec((2, 2 * count, DEPTH), lambda g: (g, 0, 0)),
        compiler_params=params(mib),
        name="spread",
    )(states)


def product_kernel(sizes, place, *refs):
    m = len(sizes)
    s_ref, (out, gg, tt, late, sem) = refs[m], refs[-5:]
    nt = (((1,), (1,)), ((), ()))
    starts = [sum(sizes[:i]) for i in range(m + 1)]
    held, copies = list(refs[:2]), [None, None]
    for i in range(2, m):
        held.append(late.at[pl.ds(starts[i] - starts[2], sizes[i])])
        copies.append(pltpu.make_async_copy(refs[i], held[i], sem.at[i - 2]))
    for copy in copies[2:]:
        copy.start()
    s = s_ref[...].reshape(192, DEPTH)
    ss = lax.dot_general(s, s, nt, preferred_element_type=F32)
    r = lax.broadcasted_iota(jnp.int32, (192, 192), 0)
    on = r == lax.broadcasted_iota(jnp.int32, (192, 192), 1)
    diag = jnp.sum(jnp.where(on, ss, 0.0), axis=0, keepdims=True)
    diag = jnp.broadcast_to(jnp.concatenate([diag, jnp.zeros((1, 64), F32)], axis=1), (8, 256))
    sub = lax.broadcasted_iota(jnp.int32, (8, 256), 0)
    lane8 = lax.broadcasted_iota(jnp.int32, (8, 256), 1)
    spare = jnp.zeros((8, 256), F32)
    for w in range(4):
        moved = pltpu.roll(diag, (SPARE + 1 - WINDOW * w) % 256, 1)
        spare = spare + jnp.where((sub == w) & (lane8 > SPARE), moved, 0.0)

    done = 0
    while done < m:
        last = done + 1
        while last < m and starts[last] - starts[done] < GROUP:
            last += 1
        a, n = starts[done], starts[last] - starts[done]
        for copy in copies[done:last]:
            if copy is not None:
                copy.wait()
        t = jnp.concatenate([ref[...] for ref in held[done:last]], axis=0).reshape(32 * n, DEPTH)
        done = last
        total = jnp.zeros((32 * n, 128), F32)
        for j in range(DEPTH // 128):
            x = t[:, 128 * j : 128 * j + 128].astype(F32)
            total = total + x * x
        at = pl.ds(32 * a, 32 * n)
        tt[at, :] = total
        even, odd = pl.ds(32 * a, 16 * n, stride=2), pl.ds(32 * a + 1, 16 * n, stride=2)
        tn = jnp.sum(tt[even, :] + tt[odd, :], axis=1, keepdims=True)
        lane = lax.broadcasted_iota(jnp.int32, (16 * n, 256), 1)
        first = lane % 2 == 0
        g = lax.dot_general(t, s, nt, preferred_element_type=F32)
        gg[0, at, :] = g[:, :128]
        gg[1, at, :] = jnp.concatenate([g[:, 128:], jnp.zeros((32 * n, 64), F32)], axis=1)
        gu, gv = (jnp.concatenate([gg[0, rows, :], gg[1, rows, :]], axis=1) for rows in (even, odd))
        both = gu + jnp.where(first, pltpu.roll(gv, 255, 1), -pltpu.roll(gv, 1, 1))
        both = jnp.where(lane < SPARE, both, jnp.where(lane == SPARE, tn, 0.0))
        both = (both.reshape(2 * n, 8, 256) + spare[None]).reshape(n, 2, 8, 256)
        for j in range(n):
            out[pl.ds(place[a + j], 1), pl.ds(place[sum(sizes) + a + j], 2)] = both[j : j + 1]


def products(at, blocks, s):
    n = len(at)
    place = jnp.stack([r for _, r, _ in at] + [4 * x + 2 * c for x, _, c in at]).astype(jnp.int32)
    out = pl.BlockSpec((4, 16, 8, 256), lambda k, place: (0, 0, 0, 0))
    return pl.pallas_call(
        functools.partial(product_kernel, [b.shape[0] for b in blocks]),
        out_shape=jax.ShapeDtypeStruct((4, 16, 8, 256), F32),
        grid_spec=pltpu.PrefetchScalarGridSpec(
            num_scalar_prefetch=1,
            grid=(1,),
            in_specs=[
                *[pl.BlockSpec(memory_space=pltpu.VMEM)] * 2,
                *[pl.BlockSpec(memory_space=pl.ANY)] * (len(blocks) - 2),
                pl.BlockSpec(memory_space=pltpu.VMEM),
            ],
            out_specs=out,
            scratch_shapes=[
                pltpu.VMEM((2, 32 * n, 128), F32),
                pltpu.VMEM((32 * n, 128), F32),
                pltpu.VMEM((n - blocks[0].shape[0] - blocks[1].shape[0], 32, DEPTH), jnp.bfloat16),
                pltpu.SemaphoreType.DMA((len(blocks) - 2,)),
            ],
        ),
        cost_estimate=pl.CostEstimate(flops=2 * 32 * n * 192 * DEPTH, bytes_accessed=64 * n * DEPTH, transcendentals=0),
        compiler_params=params(24),
        name="products",
    )(place, *blocks, s)


def per_device(train, test):
    a2a = functools.partial(lax.all_to_all, split_axis=0, concat_axis=0, tiled=True)
    x, core, row = lax.axis_index("x"), lax.axis_index("core"), lax.axis_index("row")
    held = spread(train, 60)
    t = a2a(held, "row")

    def swap(block):
        return lax.ppermute(block, "core", SWAP)

    def around(own):
        first = lax.ppermute(own, ("x", "core"), AHEAD)
        return first, lax.ppermute(own, ("x", "core"), BACK), lax.ppermute(first, ("x", "core"), AHEAD)

    stay = around(lax.dynamic_slice_in_dim(held, row, 1, 0))
    s, t, stay = lax.optimization_barrier((spread(test, 16), t, jnp.concatenate(stay)))
    s = a2a(s, "row")
    others = [(row + k) % 4 for k in (1, 2, 3)]
    come = around(jnp.concatenate([lax.dynamic_slice_in_dim(t, r, 1, 0) for r in others]))
    parts = [(t, range(4), (0,)), (stay, [row], (-1, 1, 2))] + [(b, others, (w,)) for b, w in zip(come, (-1, 1, 2))]
    entries = []
    for block, rows, ways in parts:
        for b, c, sign in ((block, core, 1 - 2 * core), (swap(block), 1 - core, 2 * core - 1)):
            entries.append((b, [((x + way * sign + 4) % 4, r, c) for way in ways for r in rows]))
    entries = [entries[i] for i in (0, 2, 1, 3, 4, 5, 6, 7, 8, 9)]
    blocks, at = [b for b, _ in entries], [place for _, places in entries for place in places]
    pieces = products(at, blocks, s)
    parts = a2a(pieces.reshape(32, 16, 256), ("row", "y"))
    total = jnp.sum(parts, axis=0)
    total = total + lax.ppermute(total, "zhi", SWAP)
    power = jnp.sum((total[:, :SPARE] ** 2).reshape(16, 96, 2), axis=2)
    tn = total[:, SPARE : SPARE + 1]
    diag = total[:4, SPARE + 1 :].reshape(4 * WINDOW)[:192]
    sn = jnp.sum(diag.reshape(1, 96, 2), axis=2)
    block = float(AMPS) * power / (tn * sn)
    full = a2a(jnp.broadcast_to(block[None], (8, 16, 96)), "y")
    return full.reshape(128, 96)


def solution(mesh):
    axes = ("row", "x", "core", "zhi", "y")
    fine = Mesh(mesh.devices.reshape(4, 4, 2, 2, 8), axes)
    placed = (
        P(("row", "x", "core"), None, DEV),
        P(("x", "core", "row"), None, DEV),
    )
    return jax.shard_map(
        per_device, mesh=fine, in_specs=placed, out_specs=P("row", ("x", "core")), check_vma=False
    )
```

```python
import functools

import jax
import jax.numpy as jnp
from jax import lax
from jax.experimental import pallas as pl
from jax.experimental.pallas import tpu as pltpu
from jax.sharding import Mesh, PartitionSpec as P

AMPS = 262144
F32 = jnp.float32
DEV = ("zhi", "y")
SPARE = 192
WINDOW = 63

GROUP = 7
DEPTH = 4096
SWAP = [(0, 1), (1, 0)]
AHEAD, BACK = ([(2 * x + c, 2 * ((x + way[c]) % 4) + c) for x in range(4) for c in (0, 1)] for way in ((1, -1), (-1, 1)))


def params(mib):
    return pltpu.CompilerParams(vmem_limit_bytes=mib * 1024 * 1024)


def spread_kernel(states, out):
    for j in range(out.shape[0]):
        out[j] = states[:, :, DEPTH * j : DEPTH * (j + 1)].reshape(out.shape[1:])


def spread(states, mib):
    count = states.shape[0]
    return pl.pallas_call(
        spread_kernel,
        out_shape=jax.ShapeDtypeStruct((4, 2 * count, DEPTH), states.dtype),
        grid=(2,),
        in_specs=[pl.BlockSpec((count, 2, 2 * DEPTH), lambda g: (0, 0, g))],
        out_specs=pl.BlockSpec((2, 2 * count, DEPTH), lambda g: (g, 0, 0)),
        compiler_params=params(mib),
        name="spread",
    )(states)


def product_kernel(sizes, place, *refs):
    m = len(sizes)
    s_ref, (out, gg, tt, late, sem) = refs[m], refs[-5:]
    nt = (((1,), (1,)), ((), ()))
    starts = [sum(sizes[:i]) for i in range(m + 1)]
    held, copies = list(refs[:2]), [None, None]
    for i in range(2, m):
        held.append(late.at[pl.ds(starts[i] - starts[2], sizes[i])])
        copies.append(pltpu.make_async_copy(refs[i], held[i], sem.at[i - 2]))
    for copy in copies[2:6]:
        copy.start()
    s = s_ref[...].reshape(192, DEPTH)
    ss = lax.dot_general(s, s, nt, preferred_element_type=F32)
    r = lax.broadcasted_iota(jnp.int32, (192, 192), 0)
    on = r == lax.broadcasted_iota(jnp.int32, (192, 192), 1)
    diag = jnp.sum(jnp.where(on, ss, 0.0), axis=0, keepdims=True)
    diag = jnp.broadcast_to(jnp.concatenate([diag, jnp.zeros((1, 64), F32)], axis=1), (8, 256))
    sub = lax.broadcasted_iota(jnp.int32, (8, 256), 0)
    lane8 = lax.broadcasted_iota(jnp.int32, (8, 256), 1)
    spare = jnp.zeros((8, 256), F32)
    for w in range(4):
        moved = pltpu.roll(diag, (SPARE + 1 - WINDOW * w) % 256, 1)
        spare = spare + jnp.where((sub == w) & (lane8 > SPARE), moved, 0.0)

    done = 0
    while done < m:
        last = done + 1
        while last < m and starts[last] - starts[done] < GROUP:
            last += 1
        a, n = starts[done], starts[last] - starts[done]
        for copy in copies[done:last]:
            if copy is not None:
                copy.wait()
        t = jnp.concatenate([ref[...] for ref in held[done:last]], axis=0).reshape(32 * n, DEPTH)
        done = last
        total = jnp.zeros((32 * n, 128), F32)
        for j in range(DEPTH // 128):
            x = t[:, 128 * j : 128 * j + 128].astype(F32)
            total = total + x * x
        at = pl.ds(32 * a, 32 * n)
        tt[at, :] = total
        even, odd = pl.ds(32 * a, 16 * n, stride=2), pl.ds(32 * a + 1, 16 * n, stride=2)
        tn = jnp.sum(tt[even, :] + tt[odd, :], axis=1, keepdims=True)
        lane = lax.broadcasted_iota(jnp.int32, (16 * n, 256), 1)
        first = lane % 2 == 0
        g = lax.dot_general(t, s, nt, preferred_element_type=F32)
        gg[0, at, :] = g[:, :128]
        gg[1, at, :] = jnp.concatenate([g[:, 128:], jnp.zeros((32 * n, 64), F32)], axis=1)
        gu, gv = (jnp.concatenate([gg[0, rows, :], gg[1, rows, :]], axis=1) for rows in (even, odd))
        both = gu + jnp.where(first, pltpu.roll(gv, 255, 1), -pltpu.roll(gv, 1, 1))
        both = jnp.where(lane < SPARE, both, jnp.where(lane == SPARE, tn, 0.0))
        both = (both.reshape(2 * n, 8, 256) + spare[None]).reshape(n, 2, 8, 256)
        for j in range(n):
            out[pl.ds(place[a + j], 1), pl.ds(place[sum(sizes) + a + j], 2)] = both[j : j + 1]
        if a == 0:
            for copy in copies[6:]:
                copy.start()


def products(at, blocks, s):
    n = len(at)
    place = jnp.stack([r for _, r, _ in at] + [4 * x + 2 * c for x, _, c in at]).astype(jnp.int32)
    out = pl.BlockSpec((4, 16, 8, 256), lambda k, place: (0, 0, 0, 0))
    return pl.pallas_call(
        functools.partial(product_kernel, [b.shape[0] for b in blocks]),
        out_shape=jax.ShapeDtypeStruct((4, 16, 8, 256), F32),
        grid_spec=pltpu.PrefetchScalarGridSpec(
            num_scalar_prefetch=1,
            grid=(1,),
            in_specs=[
                *[pl.BlockSpec(memory_space=pltpu.VMEM)] * 2,
                *[pl.BlockSpec(memory_space=pl.ANY)] * (len(blocks) - 2),
                pl.BlockSpec(memory_space=pltpu.VMEM),
            ],
            out_specs=out,
            scratch_shapes=[
                pltpu.VMEM((2, 32 * n, 128), F32),
                pltpu.VMEM((32 * n, 128), F32),
                pltpu.VMEM((n - blocks[0].shape[0] - blocks[1].shape[0], 32, DEPTH), jnp.bfloat16),
                pltpu.SemaphoreType.DMA((len(blocks) - 2,)),
            ],
        ),
        cost_estimate=pl.CostEstimate(flops=2 * 32 * n * 192 * DEPTH, bytes_accessed=64 * n * DEPTH, transcendentals=0),
        compiler_params=params(24),
        name="products",
    )(place, *blocks, s)


def per_device(train, test):
    a2a = functools.partial(lax.all_to_all, split_axis=0, concat_axis=0, tiled=True)
    x, core, row = lax.axis_index("x"), lax.axis_index("core"), lax.axis_index("row")
    held = spread(train, 60)
    t = a2a(held, "row")

    def swap(block):
        return lax.ppermute(block, "core", SWAP)

    def around(own):
        first = lax.ppermute(own, ("x", "core"), AHEAD)
        return first, lax.ppermute(own, ("x", "core"), BACK), lax.ppermute(first, ("x", "core"), AHEAD)

    stay = around(lax.dynamic_slice_in_dim(held, row, 1, 0))
    s, t, stay = lax.optimization_barrier((spread(test, 16), t, jnp.concatenate(stay)))
    s = a2a(s, "row")
    others = [(row + k) % 4 for k in (1, 2, 3)]
    come = around(jnp.concatenate([lax.dynamic_slice_in_dim(t, r, 1, 0) for r in others]))
    parts = [(t, range(4), (0,)), (stay, [row], (-1, 1, 2))] + [(b, others, (w,)) for b, w in zip(come, (-1, 1, 2))]
    entries = []
    for block, rows, ways in parts:
        for b, c, sign in ((block, core, 1 - 2 * core), (swap(block), 1 - core, 2 * core - 1)):
            entries.append((b, [((x + way * sign + 4) % 4, r, c) for way in ways for r in rows]))
    entries = [entries[i] for i in (0, 2, 1, 3, 4, 5, 6, 7, 8, 9)]
    blocks, at = [b for b, _ in entries], [place for _, places in entries for place in places]
    pieces = products(at, blocks, s)
    parts = a2a(pieces.reshape(32, 16, 256), ("row", "y"))
    total = jnp.sum(parts, axis=0)
    total = total + lax.ppermute(total, "zhi", SWAP)
    power = jnp.sum((total[:, :SPARE] ** 2).reshape(16, 96, 2), axis=2)
    tn = total[:, SPARE : SPARE + 1]
    diag = total[:4, SPARE + 1 :].reshape(4 * WINDOW)[:192]
    sn = jnp.sum(diag.reshape(1, 96, 2), axis=2)
    block = float(AMPS) * power / (tn * sn)
    full = a2a(jnp.broadcast_to(block[None], (8, 16, 96)), "y")
    return full.reshape(128, 96)


def solution(mesh):
    axes = ("row", "x", "core", "zhi", "y")
    fine = Mesh(mesh.devices.reshape(4, 4, 2, 2, 8), axes)
    placed = (
        P(("row", "x", "core"), None, DEV),
        P(("x", "core", "row"), None, DEV),
    )
    return jax.shard_map(
        per_device, mesh=fine, in_specs=placed, out_specs=P("row", ("x", "core")), check_vma=False
    )
```
